128 devices in a mesh: bulk: 8 (over x, core), wide: 16 (over y, z).
Axes of the slice: x: 4, y: 4, z: 4, core: 2. Of those that a mesh axis runs over, the one named last changes fastest.
Arguments:
- held: float32 [4096, 128, 256], P(('bulk', 'wide')), as said below
- source_slot: int32 [2048], P(('bulk', 'wide')), may hold values from 0 to 31, as said below
Outputs:
- q_factor: float32 [262144, 256], P(('bulk', 'wide'))
- r_factor: float32 [256, 256], replicated
The draws below stay inside these ranges and needn't reach their ends.
Inputs may be any that keep to these rules, and one draw needn't show every extreme that they name: `source_slot`: for each slab the 16 entries are distinct; one value of c = entry // 4 is used by 4 blocks, six others by two blocks each (entries c * 4 and c * 4 + 1). Slots of held that no entry of source_slot names are zero.
All inputs are finite; a program needn't handle non-finite values.
Results may differ from the reference program's by a relative error of at most 0.000073.
Values sent between devices are 32-bit elements; how exact they have to be, the bound alone decides.
A program may use at most 64 MiB of HBM per device.

```python
import math
import jax
import jax.numpy as jnp
from jax import lax

K = 256
BLK = 128
BPD = 16
CP = 4
W = 8
SLABS = 128
ROWS = 262144


def layout(key):
    base = jax.random.fold_in(key, 11)
    keys_a = jax.random.split(jax.random.fold_in(base, 1), SLABS)
    keys_b = jax.random.split(jax.random.fold_in(base, 2), SLABS)
    values = jax.vmap(lambda kk: jax.random.permutation(kk, W))(keys_a)
    order = jax.vmap(lambda kk: jax.random.permutation(kk, BPD))(keys_b)
    pair = order // 2
    within = order % 2
    pick = jnp.where(pair == 1, 0, pair)
    group = jnp.take_along_axis(values, pick, axis=1)
    inner = jnp.where(pair == 1, 2 + within, within)
    return (group * CP + inner).astype(jnp.int32)


def draw_source_slot(key, part):
    return layout(key).reshape(SLABS * BPD)


def draw_held(key, part):
    slots = layout(key)
    names = jnp.arange(W * CP, dtype=jnp.int32)
    named = jnp.any(slots[:, :, None] == names[None, None, :], axis=1)
    holder = jnp.arange(SLABS, dtype=jnp.int32)[:, None]
    owner_slab = (holder - names[None, :] // CP) % SLABS
    columns = jnp.broadcast_to(names[None, :], owner_slab.shape)
    filled = named[owner_slab, columns].astype(jnp.float32).reshape(-1)
    mixed = jax.random.fold_in(key, 23)
    key_one, key_two, key_three = jax.random.split(mixed, 3)
    shape = (SLABS * W * CP, BLK, K)
    noise = jax.random.normal(key_one, shape, jnp.float32)
    top = math.log(10.0)
    row_scale = jnp.exp(jax.random.uniform(key_two, (SLABS * W * CP, BLK, 1), jnp.float32, 0.0, top))
    col_scale = jnp.exp(jax.random.uniform(key_three, (1, 1, K), jnp.float32, 0.0, top))
    rising = jnp.exp(math.log(3.0) * jnp.arange(SLABS, dtype=jnp.float32) / max(SLABS - 1, 1))
    rising = jnp.repeat(rising, W * CP)
    return noise * row_scale * col_scale * (rising * filled)[:, None, None]


def setup_inputs(seed: int = 0) -> dict:
    keys = jax.random.split(jax.random.key(seed), 3)
    held = draw_held(jax.random.fold_in(keys[2], 71), 0)
    source_slot = draw_source_slot(jax.random.fold_in(keys[2], 71), 0)
    return dict(held=held, source_slot=source_slot)


def reference(held, source_slot):
    slots = source_slot.reshape(SLABS, BPD)
    slab_ids = jnp.arange(SLABS, dtype=jnp.int32)[:, None]
    holder = (slab_ids + slots // CP) % SLABS
    index = (holder * (W * CP) + slots).reshape(-1).astype(jnp.int32)
    matrix = held[index].reshape(SLABS * BPD * BLK, K)
    gram = jnp.dot(matrix.T.astype(jnp.float32), matrix.astype(jnp.float32), precision=lax.Precision.HIGHEST, preferred_element_type=jnp.float32) / ROWS
    r_factor = jnp.linalg.cholesky(gram).T
    q_factor = jax.scipy.linalg.solve_triangular(r_factor, matrix.T, trans=1, lower=False).T
    return (q_factor, r_factor)
```

```python
import functools

import jax
import jax.numpy as jnp
from jax import lax
from jax.experimental import pallas as pl
from jax.experimental.pallas import tpu as pltpu
from jax.sharding import PartitionSpec as P

CP = 4
W = 8
KEPT = 2
MESH = pl.DeviceIdType.MESH
TILE = 8
HALF = 128
F32 = jnp.float32
BF16 = jnp.bfloat16


def row_of(x, r):
    return jnp.broadcast_to(x[r : r + 1, :], x.shape)


def col_of(x, c):
    return jnp.broadcast_to(x[:, c : c + 1], x.shape)


def reciprocal(x):
    y = pl.reciprocal(x, approx=True)
    return y * (2.0 - x * y)


def panels(a):
    count = HALF // TILE
    a = list(a)
    sub = lax.broadcasted_iota(jnp.int32, (TILE, HALF), 0)
    lane = lax.broadcasted_iota(jnp.int32, (TILE, HALF), 1)
    e = [jnp.where(lane == sub + TILE * t, 1.0, 0.0) for t in range(count)]
    upper, inverse = [], []
    for p in range(count):
        at = TILE * p
        cols = [col_of(a[p], at + q) for q in range(TILE)]
        d = {(i, j): row_of(cols[j], i) for i in range(TILE) for j in range(i, TILE)}
        y, z, l, inv = [], [], {}, []
        for r in range(TILE):
            yr, zr = row_of(a[p], r), row_of(e[p], r)
            for q in range(r):
                yr = yr - l[r, q] * y[q]
                zr = zr - l[r, q] * z[q]
            y.append(yr)
            z.append(zr)
            inv.append(reciprocal(d[r, r]))
            for i in range(r + 1, TILE):
                l[i, r] = d[r, i] * inv[r]
            for i in range(r + 1, TILE):
                for j in range(i, TILE):
                    d[i, j] = d[i, j] - l[i, r] * d[r, j]
        scale = lax.rsqrt(d[0, 0])
        rows_y, rows_z = y[0] * scale, z[0] * scale
        for r in range(1, TILE):
            scale = lax.rsqrt(d[r, r])
            rows_y = jnp.where(sub == r, y[r] * scale, rows_y)
            rows_z = jnp.where(sub == r, z[r] * scale, rows_z)
        upper.append(jnp.where(lane >= sub + at, rows_y, 0.0))
        inverse.append(jnp.where(lane <= sub + at, rows_z, 0.0))
        y = [y[r] * inv[r] for r in range(TILE)]
        z = [z[r] * inv[r] for r in range(TILE)]
        if p + 1 < count:
            c = [col_of(a[p + 1], at + q) for q in range(TILE)]
            for r in range(TILE):
                for q in range(r):
                    c[r] = c[r] - l[r, q] * c[q]
            for r in range(TILE):
                a[p + 1] = a[p + 1] - c[r] * y[r]
                e[p + 1] = e[p + 1] - c[r] * z[r]
        if p + 2 < count:
            for r in reversed(range(TILE)):
                for q in range(r + 1, TILE):
                    y[r] = y[r] - l[q, r] * y[q]
                    z[r] = z[r] - l[q, r] * z[q]
            for t in range(p + 2, count):
                c = [col_of(a[t], at + q) for q in range(TILE)]
                for r in range(TILE):
                    a[t] = a[t] - c[r] * y[r]
                    e[t] = e[t] - c[r] * z[r]
    return upper, inverse


def dot(x, y, over):
    return lax.dot_general(
        x, y, (over, ((), ())), precision=lax.Precision.HIGHEST, preferred_element_type=F32
    )


def split(x):
    high = x.astype(BF16)
    return high, (x - high.astype(F32)).astype(BF16)


def half_dot(x, y, over):
    return lax.dot_general(x, y, (over, ((), ())), preferred_element_type=F32)


def factored(gram, r_ref, w_ref, work, cross, between):
    n = HALF
    work[...] = gram[0:n, 0:n]
    r_ref[n:, 0:n] = jnp.zeros((n, n), F32)
    w_ref[0:n, n:] = jnp.zeros((n, n), F32)

    def half(h, carry):
        up, inv = panels([work[TILE * t : TILE * (t + 1), :] for t in range(n // TILE)])

        @pl.when(h == 0)
        def _():
            for t in range(n // TILE):
                r_ref[TILE * t : TILE * (t + 1), 0:n] = up[t]
                w_ref[TILE * t : TILE * (t + 1), 0:n] = inv[t]
            w = w_ref[0:n, 0:n]
            right = dot(w, gram[0:n, n:], ((1,), (0,)))
            r_ref[0:n, n:] = right
            work[...] = gram[n:, n:] - dot(right, right, ((0,), (0,)))
            cross[...] = dot(right, w, ((0,), (0,)))
            between()

        @pl.when(h == 1)
        def _():
            for t in range(n // TILE):
                r_ref[n + TILE * t : n + TILE * (t + 1), n:] = up[t]
                w_ref[n + TILE * t : n + TILE * (t + 1), n:] = inv[t]
            w_ref[n:, 0:n] = -dot(w_ref[n:, n:], cross[...], ((1,), (0,)))

        return carry

    lax.fori_loop(0, 2, half, 0)


def window(
    bulk, wide, total,
    held, got, r_ref, w_ref,
    own, acc, parts, shares, gram, flat, work, cross, once, twice, thrice,
    load_sem, part_send, part_recv, share_send, share_recv, gram_send, gram_recv,
    slab_send, slab_recv, tree_send, tree_recv, keep_sem,
):
    my_bulk, my_wide = lax.axis_index("bulk"), lax.axis_index("wide")
    me = my_bulk * wide + my_wide
    devices = bulk * wide

    def along_wide(o):
        return (my_bulk, lax.rem(my_wide + o, wide))

    def along_bulk(o):
        return (lax.rem(my_bulk + o, bulk), my_wide)

    def behind(c):
        to = lax.rem(me + devices - c, devices)
        return (to // wide, lax.rem(to, wide))

    def remote(src, dst, send, recv, to):
        return pltpu.make_async_remote_copy(
            src_ref=src, dst_ref=dst, send_sem=send, recv_sem=recv, device_id=to, device_id_type=MESH
        )

    loads = [
        pltpu.make_async_copy(held.at[pl.ds(c * CP, CP)], own.at[pl.ds(c * CP, CP)], load_sem.at[c])
        for c in range(W)
    ]
    for load in loads:
        load.start()

    barrier = pltpu.get_barrier_semaphore()
    peers = [along_wide(o) for o in range(1, wide)] + [along_bulk(o) for o in range(1, bulk)]
    peers += [behind(c) for c in range(1, W)] + [behind(devices - c) for c in range(1, W)]
    for peer in peers:
        pl.semaphore_signal(barrier, inc=1, device_id=peer, device_id_type=MESH)
    pl.semaphore_wait(barrier, len(peers))

    first = [
        remote(
            held.at[pl.ds((2 * j + 1) * CP + KEPT, CP - KEPT)], once.at[j],
            tree_send.at[j], tree_recv.at[j], behind(1),
        )
        for j in range(W // 2)
    ]
    for copy in first:
        copy.start()
    straight = [
        remote(
            held.at[pl.ds(c * CP, KEPT)], got.at[pl.ds(c * KEPT, KEPT)],
            slab_send.at[c], slab_recv.at[c], behind(c),
        )
        for c in range(1, W)
    ]
    for copy in straight:
        copy.start()
    keep = pltpu.make_async_copy(held.at[pl.ds(0, KEPT)], got.at[pl.ds(0, KEPT)], keep_sem.at[0])
    keep.start()

    rows, k = CP * own.shape[1], own.shape[2]
    square, mixed = jnp.zeros((k, k), F32), jnp.zeros((k, k), F32)
    for c in range(W):
        loads[c].wait()
        high, low = split(own[c * CP : (c + 1) * CP].reshape(rows, k))
        square += half_dot(high, high, ((0,), (0,))) + half_dot(low, low, ((0,), (0,)))
        mixed += half_dot(high, low, ((0,), (0,)))
    acc[...] = (square + mixed + mixed.T).reshape(acc.shape)

    copies = [
        remote(acc.at[along_wide(o)[1]], parts.at[o], part_send.at[o], part_recv.at[o], along_wide(o))
        for o in range(1, wide)
    ]
    for copy in copies:
        copy.start()
    share = acc[my_wide]
    for o in range(1, wide):
        copies[o - 1].wait_recv()
        share += parts[o]
    shares[my_bulk] = share
    for copy in copies:
        copy.wait_send()
    copies = [
        remote(shares.at[my_bulk], shares.at[my_bulk], share_send.at[o], share_recv.at[o], along_bulk(o))
        for o in range(1, bulk)
    ]
    for copy in copies:
        copy.start()
    for copy in copies:
        copy.wait()
    share = shares[0]
    for b in range(1, bulk):
        share += shares[b]
    gram[my_wide] = share
    copies = [
        remote(gram.at[my_wide], gram.at[my_wide], gram_send.at[o], gram_recv.at[o], along_wide(o))
        for o in range(1, wide)
    ]
    for copy in copies:
        copy.start()
    for copy in copies:
        copy.wait()
    flat[...] = gram[...].reshape(k, k) / total

    def joined(j, c):
        return own[c * CP + KEPT : (c + 1) * CP] + once[j]

    for copy in first:
        copy.wait()
    second = [
        remote(once.at[2 * j + 1], twice.at[j], tree_send.at[4 + j], tree_recv.at[4 + j], behind(2))
        for j in range(W // 4)
    ]
    for j in range(W // 2):
        once[j] = joined(j, 2 * j)
    for copy in second:
        copy.start()
    third = remote(once.at[2], thrice, tree_send.at[6], tree_recv.at[6], behind(4))

    def between():
        for copy in second:
            copy.wait()
        once[2] = once[2] + twice[1]
        once[0] = once[0] + twice[0]
        third.start()

    factored(flat, r_ref, w_ref, work, cross, between)

    third.wait()
    once[0] = once[0] + thrice[...]
    last = pltpu.make_async_copy(once.at[0], got.at[pl.ds(W * KEPT, CP - KEPT)], keep_sem.at[1])
    last.start()
    for copy in straight:
        copy.wait()
    keep.wait()
    last.wait()


def moved_and_factored(held, total):
    bulk, wide = lax.axis_size("bulk"), lax.axis_size("wide")
    slots, blk, k = held.shape
    rest = CP - KEPT
    vmem, dma = pltpu.VMEM, pltpu.SemaphoreType.DMA
    return pl.pallas_call(
        functools.partial(window, bulk, wide, total),
        out_shape=[
            jax.ShapeDtypeStruct((W * KEPT + rest, blk, k), F32),
            jax.ShapeDtypeStruct((k, k), F32),
            jax.ShapeDtypeStruct((k, k), F32),
        ],
        in_specs=[pl.BlockSpec(memory_space=pltpu.HBM)],
        out_specs=[
            pl.BlockSpec(memory_space=pl.ANY),
            pl.BlockSpec(memory_space=vmem),
            pl.BlockSpec(memory_space=vmem),
        ],
        scratch_shapes=[
            vmem((slots, blk, k), F32),
            vmem((wide, k // wide, k), F32),
            vmem((wide, k // wide, k), F32),
            vmem((bulk, k // wide, k), F32),
            vmem((wide, k // wide, k), F32),
            vmem((k, k), F32),
            vmem((HALF, HALF), F32),
            vmem((HALF, HALF), F32),
            vmem((W // 2, rest, blk, k), F32),
            vmem((W // 4, rest, blk, k), F32),
            vmem((rest, blk, k), F32),
            dma((W,)), dma((wide,)), dma((wide,)), dma((bulk,)), dma((bulk,)), dma((wide,)), dma((wide,)),
            dma((W,)), dma((W,)), dma((W,)), dma((W,)), dma((2,)),
        ],
        compiler_params=pltpu.CompilerParams(
            collective_id=0, has_side_effects=True, vmem_limit_bytes=40 * 2**20
        ),
        name="window",
    )(held)


GROUP = 4


def solve_kernel(slot, got, w_ref, q_ref, w_high, w_low):
    step = pl.program_id(0)
    rest = CP - KEPT

    @pl.when(step == 0)
    def _():
        w_high[...], w_low[...] = split(w_ref[...])

    blocks = []
    for g in range(GROUP):
        s = slot[step * GROUP + g]
        c, i = s // CP, lax.rem(s, CP)
        blocks.append(got[jnp.where(i < KEPT, c * KEPT + i, W * KEPT + i - KEPT)])
    high, low = split(jnp.concatenate(blocks, axis=0))
    over = ((1,), (1,))
    q_ref[...] = (
        half_dot(low, w_high[...], over) + half_dot(high, w_low[...], over) + half_dot(high, w_high[...], over)
    )


def solved(got, w, source_slot):
    count, (_, blk, k) = source_slot.shape[0], got.shape
    return pl.pallas_call(
        solve_kernel,
        grid_spec=pltpu.PrefetchScalarGridSpec(
            num_scalar_prefetch=1,
            grid=(count // GROUP,),
            in_specs=[
                pl.BlockSpec(got.shape, lambda i, s: (0, 0, 0)),
                pl.BlockSpec((k, k), lambda i, s: (0, 0)),
            ],
            out_specs=pl.BlockSpec((GROUP * blk, k), lambda i, s: (i, 0)),
            scratch_shapes=[pltpu.VMEM((k, k), BF16), pltpu.VMEM((k, k), BF16)],
        ),
        out_shape=jax.ShapeDtypeStruct((count * blk, k), F32),
        compiler_params=pltpu.CompilerParams(vmem_limit_bytes=24 * 2**20),
        name="solve",
    )(source_slot, got, w)


def local(held, source_slot):
    total = lax.axis_size("bulk") * lax.axis_size("wide") * source_slot.shape[0] * held.shape[1]
    got, r_factor, w = moved_and_factored(held, total)
    return (solved(got, w, source_slot), r_factor)


def solution(mesh):
    in_specs = (P(("bulk", "wide"), None, None), P(("bulk", "wide")))
    out_specs = (P(("bulk", "wide"), None), P())
    return jax.shard_map(local, mesh=mesh, in_specs=in_specs, out_specs=out_specs, check_vma=False)
```

```python
import functools

import jax
import jax.numpy as jnp
from jax import lax
from jax.experimental import pallas as pl
from jax.experimental.pallas import tpu as pltpu
from jax.sharding import PartitionSpec as P

CP = 4
W = 8
KEPT = 2
EARLY, LATE = (7, 6, 5, 4), (3, 2, 1)
ROW_AT = 0
VMEM = 40 * 2**20
MESH = pl.DeviceIdType.MESH
TILE = 8
HALF = 128
F32 = jnp.float32
BF16 = jnp.bfloat16


def row_of(x, r):
    return jnp.broadcast_to(x[r : r + 1, :], x.shape)


def col_of(x, c):
    return jnp.broadcast_to(x[:, c : c + 1], x.shape)


def reciprocal(x):
    y = pl.reciprocal(x, approx=True)
    return y * (2.0 - x * y)


def panels(a):
    count = HALF // TILE
    a = list(a)
    sub = lax.broadcasted_iota(jnp.int32, (TILE, HALF), 0)
    lane = lax.broadcasted_iota(jnp.int32, (TILE, HALF), 1)
    e = [jnp.where(lane == sub + TILE * t, 1.0, 0.0) for t in range(count)]
    upper, inverse = [], []
    for p in range(count):
        at = TILE * p
        cols = [col_of(a[p], at + q) for q in range(TILE)]
        d = {(i, j): row_of(cols[j], i) for i in range(TILE) for j in range(i, TILE)}
        y, z, l, inv = [], [], {}, []
        for r in range(TILE):
            yr, zr = row_of(a[p], r), row_of(e[p], r)
            for q in range(r):
                yr = yr - l[r, q] * y[q]
                zr = zr - l[r, q] * z[q]
            y.append(yr)
            z.append(zr)
            inv.append(reciprocal(d[r, r]))
            for i in range(r + 1, TILE):
                l[i, r] = d[r, i] * inv[r]
            for i in range(r + 1, TILE):
                for j in range(i, TILE):
                    d[i, j] = d[i, j] - l[i, r] * d[r, j]
        scale = lax.rsqrt(d[0, 0])
        rows_y, rows_z = y[0] * scale, z[0] * scale
        for r in range(1, TILE):
            scale = lax.rsqrt(d[r, r])
            rows_y = jnp.where(sub == r, y[r] * scale, rows_y)
            rows_z = jnp.where(sub == r, z[r] * scale, rows_z)
        upper.append(jnp.where(lane >= sub + at, rows_y, 0.0))
        inverse.append(jnp.where(lane <= sub + at, rows_z, 0.0))
        y = [y[r] * inv[r] for r in range(TILE)]
        z = [z[r] * inv[r] for r in range(TILE)]
        if p + 1 < count:
            c = [col_of(a[p + 1], at + q) for q in range(TILE)]
            for r in range(TILE):
                for q in range(r):
                    c[r] = c[r] - l[r, q] * c[q]
            for r in range(TILE):
                a[p + 1] = a[p + 1] - c[r] * y[r]
                e[p + 1] = e[p + 1] - c[r] * z[r]
        if p + 2 < count:
            for r in reversed(range(TILE)):
                for q in range(r + 1, TILE):
                    y[r] = y[r] - l[q, r] * y[q]
                    z[r] = z[r] - l[q, r] * z[q]
            for t in range(p + 2, count):
                c = [col_of(a[t], at + q) for q in range(TILE)]
                for r in range(TILE):
                    a[t] = a[t] - c[r] * y[r]
                    e[t] = e[t] - c[r] * z[r]
    return upper, inverse


def dot(x, y, over):
    return lax.dot_general(
        x, y, (over, ((), ())), precision=lax.Precision.HIGHEST, preferred_element_type=F32
    )


def split(x):
    high = x.astype(BF16)
    return high, (x - high.astype(F32)).astype(BF16)


def half_dot(x, y, over):
    return lax.dot_general(x, y, (over, ((), ())), preferred_element_type=F32)


def factored(gram, r_ref, w_ref, work, cross, between):
    n = HALF
    work[...] = gram[0:n, 0:n]
    r_ref[n:, 0:n] = jnp.zeros((n, n), F32)
    w_ref[0:n, n:] = jnp.zeros((n, n), F32)

    def half(h, carry):
        up, inv = panels([work[TILE * t : TILE * (t + 1), :] for t in range(n // TILE)])

        @pl.when(h == 0)
        def _():
            for t in range(n // TILE):
                r_ref[TILE * t : TILE * (t + 1), 0:n] = up[t]
                w_ref[TILE * t : TILE * (t + 1), 0:n] = inv[t]
            w = w_ref[0:n, 0:n]
            right = dot(w, gram[0:n, n:], ((1,), (0,)))
            r_ref[0:n, n:] = right
            work[...] = gram[n:, n:] - dot(right, right, ((0,), (0,)))
            cross[...] = dot(right, w, ((0,), (0,)))
            between()

        @pl.when(h == 1)
        def _():
            for t in range(n // TILE):
                r_ref[n + TILE * t : n + TILE * (t + 1), n:] = up[t]
                w_ref[n + TILE * t : n + TILE * (t + 1), n:] = inv[t]
            w_ref[n:, 0:n] = -dot(w_ref[n:, n:], cross[...], ((1,), (0,)))

        return carry

    lax.fori_loop(0, 2, half, 0)


def window(
    bulk, wide, total,
    held, got, r_ref, w_ref,
    own, acc, parts, shares, gram, flat, work, cross, across, sums, down,
    load_sem, part_send, part_recv, share_send, share_recv, gram_send, gram_recv,
    slab_send, slab_recv, row_send, row_recv, down_send, down_recv, keep_sem,
):
    my_bulk, my_wide = lax.axis_index("bulk"), lax.axis_index("wide")
    me = my_bulk * wide + my_wide
    devices = bulk * wide
    column = lax.rem(my_wide, CP)

    def along_wide(o):
        return (my_bulk, lax.rem(my_wide + o, wide))

    def along_bulk(o):
        return (lax.rem(my_bulk + o, bulk), my_wide)

    def behind(c):
        to = lax.rem(me + devices - c, devices)
        return (to // wide, lax.rem(to, wide))

    def in_row(b):
        return (my_bulk, my_wide - column + lax.rem(column + CP - b, CP))

    def remote(src, dst, send, recv, to):
        return pltpu.make_async_remote_copy(
            src_ref=src, dst_ref=dst, send_sem=send, recv_sem=recv, device_id=to, device_id_type=MESH
        )

    barrier = pltpu.get_barrier_semaphore()
    peers = [along_wide(o) for o in range(1, wide)] + [along_bulk(o) for o in range(1, bulk)]
    far = [*range(1, W), 2 * CP]
    peers += [behind(c) for c in far] + [behind(devices - c) for c in far]
    for peer in peers:
        pl.semaphore_signal(barrier, inc=1, device_id=peer, device_id_type=MESH)

    loads = [
        pltpu.make_async_copy(held.at[pl.ds(c * CP, CP)], own.at[pl.ds(c * CP, CP)], load_sem.at[c])
        for c in range(W)
    ]
    for load in loads:
        load.start()
    keep = pltpu.make_async_copy(held.at[pl.ds(0, KEPT)], got.at[pl.ds(0, KEPT)], keep_sem.at[0])
    keep.start()

    rows, k = CP * own.shape[1], own.shape[2]
    square, mixed = jnp.zeros((k, k), F32), jnp.zeros((k, k), F32)
    for c in range(W):
        loads[c].wait()
        high, low = split(own[c * CP : (c + 1) * CP].reshape(rows, k))
        square += half_dot(high, high, ((0,), (0,))) + half_dot(low, low, ((0,), (0,)))
        mixed += half_dot(high, low, ((0,), (0,)))
    acc[...] = (square + mixed + mixed.T).reshape(acc.shape)

    pl.semaphore_wait(barrier, len(peers))

    part_copies = [
        remote(acc.at[along_wide(o)[1]], parts.at[o], part_send.at[o], part_recv.at[o], along_wide(o))
        for o in range(1, wide)
    ]
    for copy in part_copies:
        copy.start()

    row_copies = [
        remote(
            held.at[pl.ds(c * CP + KEPT, CP - KEPT)], across.at[c],
            row_send.at[c], row_recv.at[c], in_row(c % CP),
        )
        for c in range(W) if c % CP
    ]
    for copy in row_copies:
        copy.start()
    straight = {
        c: remote(
            held.at[pl.ds(c * CP, KEPT)], got.at[pl.ds(c * KEPT, KEPT)],
            slab_send.at[c], slab_recv.at[c], behind(c),
        )
        for c in range(1, W)
    }
    for c in EARLY:
        straight[c].start()

    share = acc[my_wide]
    for o in range(1, wide):
        part_copies[o - 1].wait_recv()
        share += parts[o]
    shares[my_bulk] = share
    share_copies = [
        remote(shares.at[my_bulk], shares.at[my_bulk], share_send.at[o], share_recv.at[o], along_bulk(o))
        for o in range(1, bulk)
    ]
    for copy in share_copies:
        copy.start()
    for copy in part_copies:
        copy.wait_send()
    for copy in share_copies:
        copy.wait()
    share = shares[0]
    for b in range(1, bulk):
        share += shares[b]
    gram[my_wide] = share
    gram_copies = [
        remote(gram.at[my_wide], gram.at[my_wide], gram_send.at[o], gram_recv.at[o], along_wide(o))
        for o in range(1, wide)
    ]
    for copy in gram_copies:
        copy.start()
    for c in LATE:
        straight[c].start()
    for copy in gram_copies:
        copy.wait()
    flat[...] = gram[...].reshape(k, k) / total

    down_copies = [
        remote(sums.at[i], down.at[i], down_send.at[i], down_recv.at[i], behind(CP * i)) for i in (1, 2)
    ]

    def next_row():
        for copy in row_copies:
            copy.wait()
        mine = [own[KEPT:CP], own[CP * CP + KEPT : CP * CP + CP], jnp.zeros(sums.shape[1:], F32)]
        for b in range(1, CP):
            near, far = across[b], across[b + CP]
            inside = column + b < CP
            mine[0] += jnp.where(inside, near, 0.0)
            mine[1] += jnp.where(inside, far, near)
            mine[2] += jnp.where(inside, 0.0, far)
        for i in range(3):
            sums[i] = mine[i]
        for copy in down_copies:
            copy.start()

    if ROW_AT == 0:
        next_row()
    factored(flat, r_ref, w_ref, work, cross, next_row if ROW_AT == 1 else lambda: None)
    if ROW_AT == 2:
        next_row()

    for copy in down_copies:
        copy.wait()
    sums[0] = sums[0] + down[1] + down[2]
    last = pltpu.make_async_copy(sums.at[0], got.at[pl.ds(W * KEPT, CP - KEPT)], keep_sem.at[1])
    last.start()
    for c in (*EARLY, *LATE):
        straight[c].wait()
    keep.wait()
    last.wait()


def moved_and_factored(held, total):
    bulk, wide = lax.axis_size("bulk"), lax.axis_size("wide")
    slots, blk, k = held.shape
    rest = CP - KEPT
    vmem, dma = pltpu.VMEM, pltpu.SemaphoreType.DMA
    return pl.pallas_call(
        functools.partial(window, bulk, wide, total),
        out_shape=[
            jax.ShapeDtypeStruct((W * KEPT + rest, blk, k), F32),
            jax.ShapeDtypeStruct((k, k), F32),
            jax.ShapeDtypeStruct((k, k), F32),
        ],
        in_specs=[pl.BlockSpec(memory_space=pltpu.HBM)],
        out_specs=[
            pl.BlockSpec(memory_space=pl.ANY),
            pl.BlockSpec(memory_space=vmem),
            pl.BlockSpec(memory_space=vmem),
        ],
        scratch_shapes=[
            vmem((slots, blk, k), F32),
            vmem((wide, k // wide, k), F32),
            vmem((wide, k // wide, k), F32),
            vmem((bulk, k // wide, k), F32),
            vmem((wide, k // wide, k), F32),
            vmem((k, k), F32),
            vmem((HALF, HALF), F32),
            vmem((HALF, HALF), F32),
            vmem((W, rest, blk, k), F32),
            vmem((3, rest, blk, k), F32),
            vmem((3, rest, blk, k), F32),
            dma((W,)), dma((wide,)), dma((wide,)), dma((bulk,)), dma((bulk,)), dma((wide,)), dma((wide,)),
            dma((W,)), dma((W,)), dma((W,)), dma((W,)), dma((3,)), dma((3,)), dma((2,)),
        ],
        compiler_params=pltpu.CompilerParams(
            collective_id=0, has_side_effects=True, vmem_limit_bytes=VMEM
        ),
        name="window",
    )(held)


GROUP = 4


def solve_kernel(slot, got, w_ref, q_ref, w_high, w_low):
    step = pl.program_id(0)
    rest = CP - KEPT

    @pl.when(step == 0)
    def _():
        w_high[...], w_low[...] = split(w_ref[...])

    blocks = []
    for g in range(GROUP):
        s = slot[step * GROUP + g]
        c, i = s // CP, lax.rem(s, CP)
        blocks.append(got[jnp.where(i < KEPT, c * KEPT + i, W * KEPT + i - KEPT)])
    high, low = split(jnp.concatenate(blocks, axis=0))
    over = ((1,), (1,))
    q_ref[...] = (
        half_dot(low, w_high[...], over) + half_dot(high, w_low[...], over) + half_dot(high, w_high[...], over)
    )


def solved(got, w, source_slot):
    count, (_, blk, k) = source_slot.shape[0], got.shape
    return pl.pallas_call(
        solve_kernel,
        grid_spec=pltpu.PrefetchScalarGridSpec(
            num_scalar_prefetch=1,
            grid=(count // GROUP,),
            in_specs=[
                pl.BlockSpec(got.shape, lambda i, s: (0, 0, 0)),
                pl.BlockSpec((k, k), lambda i, s: (0, 0)),
            ],
            out_specs=pl.BlockSpec((GROUP * blk, k), lambda i, s: (i, 0)),
            scratch_shapes=[pltpu.VMEM((k, k), BF16), pltpu.VMEM((k, k), BF16)],
        ),
        out_shape=jax.ShapeDtypeStruct((count * blk, k), F32),
        compiler_params=pltpu.CompilerParams(vmem_limit_bytes=24 * 2**20),
        name="solve",
    )(source_slot, got, w)


def local(held, source_slot):
    total = lax.axis_size("bulk") * lax.axis_size("wide") * source_slot.shape[0] * held.shape[1]
    got, r_factor, w = moved_and_factored(held, total)
    return (solved(got, w, source_slot), r_factor)


def solution(mesh):
    in_specs = (P(("bulk", "wide"), None, None), P(("bulk", "wide")))
    out_specs = (P(("bulk", "wide"), None), P())
    return jax.shard_map(local, mesh=mesh, in_specs=in_specs, out_specs=out_specs, check_vma=False)
```

```python
import functools

import jax
import jax.numpy as jnp
from jax import lax
from jax.experimental import pallas as pl
from jax.experimental.pallas import tpu as pltpu
from jax.sharding import PartitionSpec as P

CP = 4
W = 8
KEPT = 2
def both(kind, c):
    return ((kind, c, 0), (kind, c, 1))


def rows(i, *cs):
    return tuple(("row", c, i) for c in cs)


PLAN = (
    both("slab", 4) + rows(0, 1, 3),
    (),
    (),
    rows(0, 5, 7, 2, 6) + rows(1, 1, 3, 5, 7, 2, 6)
    + both("slab", 7) + both("slab", 6) + both("slab", 5) + both("slab", 3) + both("slab", 2) + both("slab", 1),
    (),
    (),
)
ROW_AT = (1, 2)
SOLVE = (7, 6, 5, 4, 3, 2, 1, 0)
VMEM = 40 * 2**20
MESH = pl.DeviceIdType.MESH
TILE = 8
HALF = 128
F32 = jnp.float32
BF16 = jnp.bfloat16


def row_of(x, r):
    return jnp.broadcast_to(x[r : r + 1, :], x.shape)


def col_of(x, c):
    return jnp.broadcast_to(x[:, c : c + 1], x.shape)


def reciprocal(x):
    y = pl.reciprocal(x, approx=True)
    return y * (2.0 - x * y)


def panels(a):
    count = HALF // TILE
    a = list(a)
    sub = lax.broadcasted_iota(jnp.int32, (TILE, HALF), 0)
    lane = lax.broadcasted_iota(jnp.int32, (TILE, HALF), 1)
    e = [jnp.where(lane == sub + TILE * t, 1.0, 0.0) for t in range(count)]
    upper, inverse = [], []
    for p in range(count):
        at = TILE * p
        cols = [col_of(a[p], at + q) for q in range(TILE)]
        d = {(i, j): row_of(cols[j], i) for i in range(TILE) for j in range(i, TILE)}
        y, z, l, inv = [], [], {}, []
        for r in range(TILE):
            yr, zr = row_of(a[p], r), row_of(e[p], r)
            for q in range(r):
                yr = yr - l[r, q] * y[q]
                zr = zr - l[r, q] * z[q]
            y.append(yr)
            z.append(zr)
            inv.append(reciprocal(d[r, r]))
            for i in range(r + 1, TILE):
                l[i, r] = d[r, i] * inv[r]
            for i in range(r + 1, TILE):
                for j in range(i, TILE):
                    d[i, j] = d[i, j] - l[i, r] * d[r, j]
        scale = lax.rsqrt(d[0, 0])
        rows_y, rows_z = y[0] * scale, z[0] * scale
        for r in range(1, TILE):
            scale = lax.rsqrt(d[r, r])
            rows_y = jnp.where(sub == r, y[r] * scale, rows_y)
            rows_z = jnp.where(sub == r, z[r] * scale, rows_z)
        upper.append(jnp.where(lane >= sub + at, rows_y, 0.0))
        inverse.append(jnp.where(lane <= sub + at, rows_z, 0.0))
        y = [y[r] * inv[r] for r in range(TILE)]
        z = [z[r] * inv[r] for r in range(TILE)]
        if p + 1 < count:
            c = [col_of(a[p + 1], at + q) for q in range(TILE)]
            for r in range(TILE):
                for q in range(r):
                    c[r] = c[r] - l[r, q] * c[q]
            for r in range(TILE):
                a[p + 1] = a[p + 1] - c[r] * y[r]
                e[p + 1] = e[p + 1] - c[r] * z[r]
        if p + 2 < count:
            for r in reversed(range(TILE)):
                for q in range(r + 1, TILE):
                    y[r] = y[r] - l[q, r] * y[q]
                    z[r] = z[r] - l[q, r] * z[q]
            for t in range(p + 2, count):
                c = [col_of(a[t], at + q) for q in range(TILE)]
                for r in range(TILE):
                    a[t] = a[t] - c[r] * y[r]
                    e[t] = e[t] - c[r] * z[r]
    return upper, inverse


def dot(x, y, over):
    return lax.dot_general(
        x, y, (over, ((), ())), precision=lax.Precision.HIGHEST, preferred_element_type=F32
    )


def split(x):
    high = x.astype(BF16)
    return high, (x - high.astype(F32)).astype(BF16)


def half_dot(x, y, over):
    return lax.dot_general(x, y, (over, ((), ())), preferred_element_type=F32)


def factored(gram, r_ref, w_ref, work, cross, between):
    n = HALF
    work[...] = gram[0:n, 0:n]
    r_ref[n:, 0:n] = jnp.zeros((n, n), F32)
    w_ref[0:n, n:] = jnp.zeros((n, n), F32)

    def half(h, carry):
        up, inv = panels([work[TILE * t : TILE * (t + 1), :] for t in range(n // TILE)])

        @pl.when(h == 0)
        def _():
            for t in range(n // TILE):
                r_ref[TILE * t : TILE * (t + 1), 0:n] = up[t]
                w_ref[TILE * t : TILE * (t + 1), 0:n] = inv[t]
            w = w_ref[0:n, 0:n]
            right = dot(w, gram[0:n, n:], ((1,), (0,)))
            r_ref[0:n, n:] = right
            work[...] = gram[n:, n:] - dot(right, right, ((0,), (0,)))
            cross[...] = dot(right, w, ((0,), (0,)))
            between()

        @pl.when(h == 1)
        def _():
            for t in range(n // TILE):
                r_ref[n + TILE * t : n + TILE * (t + 1), n:] = up[t]
                w_ref[n + TILE * t : n + TILE * (t + 1), n:] = inv[t]
            w_ref[n:, 0:n] = -dot(w_ref[n:, n:], cross[...], ((1,), (0,)))

        return carry

    lax.fori_loop(0, 2, half, 0)


def window(
    bulk, wide, total,
    slots, held, q_ref, r_ref,
    slot, slot_sem,     w_ref, solved, own, land, acc, parts, shares, columns, chunk, gram, flat, work, cross, across, sums, down, w_high, w_low,
    load_sem, part_send, part_recv, share_send, share_recv, column_send, column_recv, piece_send, piece_recv,
    gram_send, gram_recv, slab_send, slab_recv, row_send, row_recv, down_send, down_recv,
):
    my_bulk, my_wide = lax.axis_index("bulk"), lax.axis_index("wide")
    me = my_bulk * wide + my_wide
    devices = bulk * wide
    column, row = lax.rem(my_wide, CP), my_wide // CP
    height = wide // CP

    def along_bulk(o):
        return (lax.rem(my_bulk + o, bulk), my_wide)

    def behind(c):
        to = lax.rem(me + devices - c, devices)
        return (to // wide, lax.rem(to, wide))

    def in_row(b):
        return (my_bulk, row * CP + lax.rem(column + CP - b, CP))

    def in_column(b):
        return (my_bulk, lax.rem(row + height - b, height) * CP + column)

    def remote(src, dst, send, recv, to):
        return pltpu.make_async_remote_copy(
            src_ref=src, dst_ref=dst, send_sem=send, recv_sem=recv, device_id=to, device_id_type=MESH
        )

    barrier = pltpu.get_barrier_semaphore()
    far = [*range(1, W), 2 * CP]
    peers = [behind(c) for c in far] + [behind(devices - c) for c in far]
    peers += [in_column(b) for b in range(1, height)] + [along_bulk(o) for o in range(1, bulk)]
    for peer in peers:
        pl.semaphore_signal(barrier, inc=1, device_id=peer, device_id_type=MESH)

    loads = [
        pltpu.make_async_copy(held.at[pl.ds(c * CP, CP)], own.at[pl.ds(c * CP, CP)], load_sem.at[c])
        for c in range(W)
    ]
    for load in loads:
        load.start()
    places = pltpu.make_async_copy(slots, slot, slot_sem.at[0])
    places.start()

    rows, k = CP * own.shape[1], own.shape[2]
    square, mixed = jnp.zeros((k, k), F32), jnp.zeros((k, k), F32)
    for c in range(W):
        loads[c].wait()
        high, low = split(own[c * CP : (c + 1) * CP].reshape(rows, k))
        square += half_dot(high, high, ((0,), (0,))) + half_dot(low, low, ((0,), (0,)))
        mixed += half_dot(high, low, ((0,), (0,)))
    acc[...] = (square + mixed + mixed.T).reshape(acc.shape)

    pl.semaphore_wait(barrier, len(peers))

    part_copies = [
        remote(acc.at[along_bulk(o)[0]], parts.at[o], part_send.at[o], part_recv.at[o], along_bulk(o))
        for o in range(1, bulk)
    ]
    for copy in part_copies:
        copy.start()

    large = {}
    for c in range(1, W):
        for i in range(KEPT):
            large["slab", c, i] = remote(
                held.at[c * CP + i], land.at[c * KEPT + i], slab_send.at[c, i], slab_recv.at[c, i], behind(c)
            )
            if c % CP:
                large["row", c, i] = remote(
                    held.at[c * CP + KEPT + i], across.at[c, i],
                    row_send.at[c, i], row_recv.at[c, i], in_row(c % CP),
                )

    def begin(point):
        for key in PLAN[point]:
            large[key].start()

    begin(0)

    part = acc[my_bulk]
    for o in range(1, bulk):
        part_copies[o - 1].wait_recv()
        part += parts[o]
    shares[0] = part.reshape(shares.shape[1:])
    share_copies = [
        remote(shares.at[0, lax.rem(column + CP - b, CP)], shares.at[b, 0], share_send.at[b], share_recv.at[b], in_row(b))
        for b in range(1, CP)
    ]
    for copy in share_copies:
        copy.start()
    begin(1)
    for copy in part_copies:
        copy.wait_send()
    share = shares[0, column]
    for b in range(1, CP):
        share_copies[b - 1].wait_recv()
        share += shares[b, 0]
    columns[row] = share
    column_copies = [
        remote(columns.at[row], columns.at[row], column_send.at[b], column_recv.at[b], in_column(b))
        for b in range(1, height)
    ]
    for copy in column_copies:
        copy.start()
    begin(2)
    for copy in share_copies:
        copy.wait_send()
    for copy in column_copies:
        copy.wait()
    share = columns[0]
    for b in range(1, height):
        share += columns[b]
    chunk[column] = share
    piece_copies = [
        remote(chunk.at[column], chunk.at[column], piece_send.at[b], piece_recv.at[b], in_row(b))
        for b in range(1, CP)
    ]
    for copy in piece_copies:
        copy.start()
    begin(3)
    for copy in piece_copies:
        copy.wait()
    gram[my_bulk] = chunk[...].reshape(gram.shape[1:])
    gram_copies = [
        remote(gram.at[my_bulk], gram.at[my_bulk], gram_send.at[o], gram_recv.at[o], along_bulk(o))
        for o in range(1, bulk)
    ]
    for copy in gram_copies:
        copy.start()
    begin(4)
    for copy in gram_copies:
        copy.wait()
    flat[...] = gram[...].reshape(k, k) / total

    begin(5)

    down_copies = [
        [
            remote(sums.at[i, n], down.at[i, n], down_send.at[i, n], down_recv.at[i, n], behind(CP * i))
            for i in (1, 2)
        ]
        for n in range(CP - KEPT)
    ]

    def next_row(n):
        for key, copy in large.items():
            if key[0] == "row" and key[2] == n:
                copy.wait()
        mine = [own[KEPT + n], own[CP * CP + KEPT + n], jnp.zeros(sums.shape[2:], F32)]
        for b in range(1, CP):
            near, far = across[b, n], across[b + CP, n]
            inside = column + b < CP
            mine[0] += jnp.where(inside, near, 0.0)
            mine[1] += jnp.where(inside, far, near)
            mine[2] += jnp.where(inside, 0.0, far)
        for i in range(3):
            sums[i, n] = mine[i]
        for copy in down_copies[n]:
            copy.start()

    def at_point(point):
        for n in range(CP - KEPT):
            if ROW_AT[n] == point:
                next_row(n)

    at_point(0)
    factored(flat, r_ref, w_ref, work, cross, functools.partial(at_point, 1))
    at_point(2)
    w_high[...], w_low[...] = split(w_ref[...])

    def solve(blocks, at):
        high, low = split(blocks.reshape(-1, k))
        over = ((1,), (1,))
        q = half_dot(low, w_high[...], over) + half_dot(high, w_low[...], over) + half_dot(high, w_high[...], over)
        solved[at : at + blocks.shape[0]] = q.reshape(blocks.shape)

    solve(own[0:KEPT], 0)
    for c in SOLVE:
        if c:
            for i in range(KEPT):
                large["slab", c, i].wait()
            solve(land[c * KEPT : (c + 1) * KEPT], c * KEPT)
        else:
            for n in range(CP - KEPT):
                for copy in down_copies[n]:
                    copy.wait()
            solve(sums[0] + down[1] + down[2], W * KEPT)

    places.wait()
    blk = own.shape[1]
    for j in range(q_ref.shape[0] // blk):
        c, i = slot[j] // CP, lax.rem(slot[j], CP)
        q_ref[j * blk : (j + 1) * blk] = solved[jnp.where(i < KEPT, c * KEPT + i, W * KEPT + i - KEPT)]


def moved_and_solved(held, source_slot, total):
    bulk, wide = lax.axis_size("bulk"), lax.axis_size("wide")
    slots, blk, k = held.shape
    rest = CP - KEPT
    vmem, dma = pltpu.VMEM, pltpu.SemaphoreType.DMA
    return pl.pallas_call(
        functools.partial(window, bulk, wide, total),
        out_shape=[
            jax.ShapeDtypeStruct((source_slot.shape[0] * blk, k), F32),
            jax.ShapeDtypeStruct((k, k), F32),
        ],
        in_specs=[pl.BlockSpec(memory_space=pl.ANY)] * 2,
        out_specs=[pl.BlockSpec(memory_space=vmem)] * 2,
        scratch_shapes=[
            pltpu.SMEM(source_slot.shape, jnp.int32),
            dma((1,)),
            vmem((k, k), F32),
            vmem((W * KEPT + rest, blk, k), F32),
            vmem((slots, blk, k), F32),
            vmem((W * KEPT, blk, k), F32),
            vmem((bulk, k // bulk, k), F32),
            vmem((bulk, k // bulk, k), F32),
            vmem((CP, CP, k // bulk // CP, k), F32),
            vmem((wide // CP, k // bulk // CP, k), F32),
            vmem((CP, k // bulk // CP, k), F32),
            vmem((bulk, k // bulk, k), F32),
            vmem((k, k), F32),
            vmem((HALF, HALF), F32),
            vmem((HALF, HALF), F32),
            vmem((W, rest, blk, k), F32),
            vmem((3, rest, blk, k), F32),
            vmem((3, rest, blk, k), F32),
            vmem((k, k), BF16),
            vmem((k, k), BF16),
            dma((W,)), dma((bulk,)), dma((bulk,)), dma((CP,)), dma((CP,)), dma((wide // CP,)), dma((wide // CP,)),
            dma((CP,)), dma((CP,)), dma((bulk,)), dma((bulk,)),
            dma((W, KEPT)), dma((W, KEPT)), dma((W, KEPT)), dma((W, KEPT)), dma((3, rest)), dma((3, rest)),
        ],
        compiler_params=pltpu.CompilerParams(
            collective_id=0, has_side_effects=True, vmem_limit_bytes=VMEM
        ),
        name="window",
    )(source_slot, held)


def local(held, source_slot):
    total = lax.axis_size("bulk") * lax.axis_size("wide") * source_slot.shape[0] * held.shape[1]
    return tuple(moved_and_solved(held, source_slot, total))


def solution(mesh):
    in_specs = (P(("bulk", "wide"), None, None), P(("bulk", "wide")))
    out_specs = (P(("bulk", "wide"), None), P())
    return jax.shard_map(local, mesh=mesh, in_specs=in_specs, out_specs=out_specs, check_vma=False)
```

```python
import functools

import jax
import jax.numpy as jnp
from jax import lax
from jax.experimental import pallas as pl
from jax.experimental.pallas import tpu as pltpu
from jax.sharding import PartitionSpec as P

CP = 4
W = 8
KEPT = 2
def both(kind, c):
    return ((kind, c, 0), (kind, c, 1))


def rows(i, *cs):
    return tuple(("row", c, i) for c in cs)


PLAN = (
    both("slab", 4) + rows(0, 1, 3),
    rows(0, 5, 7),
    (("slab", 7, 0),),
    rows(0, 2, 6) + rows(1, 1, 3) + (("slab", 7, 1),) + rows(1, 5, 7) + both("slab", 6) + rows(1, 2, 6)
    + both("slab", 5) + both("slab", 3) + both("slab", 1) + both("slab", 2),
    (),
    (),
)
ROW_AT = (1, 2)
SOLVE = (7, 6, 5, 4, 3, 2, 1, 0)
VMEM = 50 * 2**20
MESH = pl.DeviceIdType.MESH
TILE = 8
HALF = 128
F32 = jnp.float32
BF16 = jnp.bfloat16


def row_of(x, r):
    return jnp.broadcast_to(x[r : r + 1, :], x.shape)


def col_of(x, c):
    return jnp.broadcast_to(x[:, c : c + 1], x.shape)


def reciprocal(x):
    y = pl.reciprocal(x, approx=True)
    return y * (2.0 - x * y)


def panels(a):
    count = HALF // TILE
    a = list(a)
    sub = lax.broadcasted_iota(jnp.int32, (TILE, HALF), 0)
    lane = lax.broadcasted_iota(jnp.int32, (TILE, HALF), 1)
    e = [jnp.where(lane == sub + TILE * t, 1.0, 0.0) for t in range(count)]
    upper, inverse = [], []
    for p in range(count):
        at = TILE * p
        cols = [col_of(a[p], at + q) for q in range(TILE)]
        d = {(i, j): row_of(cols[j], i) for i in range(TILE) for j in range(i, TILE)}
        y, z, l, inv = [], [], {}, []
        for r in range(TILE):
            yr, zr = row_of(a[p], r), row_of(e[p], r)
            for q in range(r):
                yr = yr - l[r, q] * y[q]
                zr = zr - l[r, q] * z[q]
            y.append(yr)
            z.append(zr)
            inv.append(reciprocal(d[r, r]))
            for i in range(r + 1, TILE):
                l[i, r] = d[r, i] * inv[r]
            for i in range(r + 1, TILE):
                for j in range(i, TILE):
                    d[i, j] = d[i, j] - l[i, r] * d[r, j]
        scale = lax.rsqrt(d[0, 0])
        rows_y, rows_z = y[0] * scale, z[0] * scale
        for r in range(1, TILE):
            scale = lax.rsqrt(d[r, r])
            rows_y = jnp.where(sub == r, y[r] * scale, rows_y)
            rows_z = jnp.where(sub == r, z[r] * scale, rows_z)
        upper.append(jnp.where(lane >= sub + at, rows_y, 0.0))
        inverse.append(jnp.where(lane <= sub + at, rows_z, 0.0))
        y = [y[r] * inv[r] for r in range(TILE)]
        z = [z[r] * inv[r] for r in range(TILE)]
        if p + 1 < count:
            c = [col_of(a[p + 1], at + q) for q in range(TILE)]
            for r in range(TILE):
                for q in range(r):
                    c[r] = c[r] - l[r, q] * c[q]
            for r in range(TILE):
                a[p + 1] = a[p + 1] - c[r] * y[r]
                e[p + 1] = e[p + 1] - c[r] * z[r]
        if p + 2 < count:
            for r in reversed(range(TILE)):
                for q in range(r + 1, TILE):
                    y[r] = y[r] - l[q, r] * y[q]
                    z[r] = z[r] - l[q, r] * z[q]
            for t in range(p + 2, count):
                c = [col_of(a[t], at + q) for q in range(TILE)]
                for r in range(TILE):
                    a[t] = a[t] - c[r] * y[r]
                    e[t] = e[t] - c[r] * z[r]
    return upper, inverse


def dot(x, y, over):
    return lax.dot_general(
        x, y, (over, ((), ())), precision=lax.Precision.HIGHEST, preferred_element_type=F32
    )


def split(x):
    high = x.astype(BF16)
    return high, (x - high.astype(F32)).astype(BF16)


def half_dot(x, y, over):
    return lax.dot_general(x, y, (over, ((), ())), preferred_element_type=F32)


def factored(gram, r_ref, w_ref, work, cross, between):
    n = HALF
    work[...] = gram[0:n, 0:n]
    r_ref[n:, 0:n] = jnp.zeros((n, n), F32)
    w_ref[0:n, n:] = jnp.zeros((n, n), F32)

    def half(h, carry):
        up, inv = panels([work[TILE * t : TILE * (t + 1), :] for t in range(n // TILE)])

        @pl.when(h == 0)
        def _():
            for t in range(n // TILE):
                r_ref[TILE * t : TILE * (t + 1), 0:n] = up[t]
                w_ref[TILE * t : TILE * (t + 1), 0:n] = inv[t]
            w = w_ref[0:n, 0:n]
            right = dot(w, gram[0:n, n:], ((1,), (0,)))
            r_ref[0:n, n:] = right
            work[...] = gram[n:, n:] - dot(right, right, ((0,), (0,)))
            cross[...] = dot(right, w, ((0,), (0,)))
            between()

        @pl.when(h == 1)
        def _():
            for t in range(n // TILE):
                r_ref[n + TILE * t : n + TILE * (t + 1), n:] = up[t]
                w_ref[n + TILE * t : n + TILE * (t + 1), n:] = inv[t]
            w_ref[n:, 0:n] = -dot(w_ref[n:, n:], cross[...], ((1,), (0,)))

        return carry

    lax.fori_loop(0, 2, half, 0)


def window(
    bulk, wide, total,
    slots, held, q_ref, r_ref,
    slot, slot_sem,     w_ref, solved, own, land, acc, parts, shares, columns, chunk, gram, flat, work, cross, across, sums, down, w_high, w_low,
    load_sem, part_send, part_recv, share_send, share_recv, column_send, column_recv, piece_send, piece_recv,
    gram_send, gram_recv, slab_send, slab_recv, row_send, row_recv, down_send, down_recv,
):
    my_bulk, my_wide = lax.axis_index("bulk"), lax.axis_index("wide")
    me = my_bulk * wide + my_wide
    devices = bulk * wide
    column, row = lax.rem(my_wide, CP), my_wide // CP
    height = wide // CP

    def along_bulk(o):
        return (lax.rem(my_bulk + o, bulk), my_wide)

    def behind(c):
        to = lax.rem(me + devices - c, devices)
        return (to // wide, lax.rem(to, wide))

    def in_row(b):
        return (my_bulk, row * CP + lax.rem(column + CP - b, CP))

    def in_column(b):
        return (my_bulk, lax.rem(row + height - b, height) * CP + column)

    def remote(src, dst, send, recv, to):
        return pltpu.make_async_remote_copy(
            src_ref=src, dst_ref=dst, send_sem=send, recv_sem=recv, device_id=to, device_id_type=MESH
        )

    barrier = pltpu.get_barrier_semaphore()
    far = [*range(1, W), 2 * CP]
    peers = [behind(c) for c in far] + [behind(devices - c) for c in far]
    peers += [in_column(b) for b in range(1, height)] + [along_bulk(o) for o in range(1, bulk)]
    for peer in peers:
        pl.semaphore_signal(barrier, inc=1, device_id=peer, device_id_type=MESH)

    loads = [
        pltpu.make_async_copy(held.at[pl.ds(c * CP, CP)], own.at[pl.ds(c * CP, CP)], load_sem.at[c])
        for c in range(W)
    ]
    for load in loads:
        load.start()
    places = pltpu.make_async_copy(slots, slot, slot_sem.at[0])
    places.start()

    rows, k = CP * own.shape[1], own.shape[2]
    square, mixed = jnp.zeros((k, k), F32), jnp.zeros((k, k), F32)
    for c in range(W):
        loads[c].wait()
        high, low = split(own[c * CP : (c + 1) * CP].reshape(rows, k))
        square += half_dot(high, high, ((0,), (0,))) + half_dot(low, low, ((0,), (0,)))
        mixed += half_dot(high, low, ((0,), (0,)))
    acc[...] = (square + mixed + mixed.T).reshape(acc.shape)

    pl.semaphore_wait(barrier, len(peers))

    part_copies = [
        remote(acc.at[along_bulk(o)[0]], parts.at[o], part_send.at[o], part_recv.at[o], along_bulk(o))
        for o in range(1, bulk)
    ]
    for copy in part_copies:
        copy.start()

    large = {}
    for c in range(1, W):
        for i in range(KEPT):
            large["slab", c, i] = remote(
                held.at[c * CP + i], land.at[c * KEPT + i], slab_send.at[c, i], slab_recv.at[c, i], behind(c)
            )
            if c % CP:
                large["row", c, i] = remote(
                    held.at[c * CP + KEPT + i], across.at[c, i],
                    row_send.at[c, i], row_recv.at[c, i], in_row(c % CP),
                )

    def begin(point):
        for key in PLAN[point]:
            large[key].start()

    begin(0)

    part = acc[my_bulk]
    for o in range(1, bulk):
        part_copies[o - 1].wait_recv()
        part += parts[o]
    shares[0] = part.reshape(shares.shape[1:])
    share_copies = [
        remote(shares.at[0, lax.rem(column + CP - b, CP)], shares.at[b, 0], share_send.at[b], share_recv.at[b], in_row(b))
        for b in range(1, CP)
    ]
    for copy in share_copies:
        copy.start()
    begin(1)
    for copy in part_copies:
        copy.wait_send()
    share = shares[0, column]
    for b in range(1, CP):
        share_copies[b - 1].wait_recv()
        share += shares[b, 0]
    columns[row] = share
    column_copies = [
        remote(columns.at[row], columns.at[row], column_send.at[b], column_recv.at[b], in_column(b))
        for b in range(1, height)
    ]
    for copy in column_copies:
        copy.start()
    begin(2)
    for copy in share_copies:
        copy.wait_send()
    for copy in column_copies:
        copy.wait()
    share = columns[0]
    for b in range(1, height):
        share += columns[b]
    chunk[column] = share
    piece_copies = [
        remote(chunk.at[column], chunk.at[column], piece_send.at[b], piece_recv.at[b], in_row(b))
        for b in range(1, CP)
    ]
    for copy in piece_copies:
        copy.start()
    begin(3)
    for copy in piece_copies:
        copy.wait()
    gram[my_bulk] = chunk[...].reshape(gram.shape[1:])
    gram_copies = [
        remote(gram.at[my_bulk], gram.at[my_bulk], gram_send.at[o], gram_recv.at[o], along_bulk(o))
        for o in range(1, bulk)
    ]
    for copy in gram_copies:
        copy.start()
    begin(4)
    for copy in gram_copies:
        copy.wait()
    flat[...] = gram[...].reshape(k, k) / total

    begin(5)

    down_copies = [
        [
            remote(sums.at[i, n], down.at[i, n], down_send.at[i, n], down_recv.at[i, n], behind(CP * i))
            for i in (1, 2)
        ]
        for n in range(CP - KEPT)
    ]

    def next_row(n):
        for key, copy in large.items():
            if key[0] == "row" and key[2] == n:
                copy.wait()
        mine = [own[KEPT + n], own[CP * CP + KEPT + n], jnp.zeros(sums.shape[2:], F32)]
        for b in range(1, CP):
            near, far = across[b, n], across[b + CP, n]
            inside = column + b < CP
            mine[0] += jnp.where(inside, near, 0.0)
            mine[1] += jnp.where(inside, far, near)
            mine[2] += jnp.where(inside, 0.0, far)
        for i in range(3):
            sums[i, n] = mine[i]
        for copy in down_copies[n]:
            copy.start()

    def at_point(point):
        for n in range(CP - KEPT):
            if ROW_AT[n] == point:
                next_row(n)

    at_point(0)
    factored(flat, r_ref, w_ref, work, cross, functools.partial(at_point, 1))
    at_point(2)
    w_high[...], w_low[...] = split(w_ref[...])

    def solve(blocks, at):
        high, low = split(blocks.reshape(-1, k))
        over = ((1,), (1,))
        q = half_dot(low, w_high[...], over) + half_dot(high, w_low[...], over) + half_dot(high, w_high[...], over)
        solved[at : at + blocks.shape[0]] = q.reshape(blocks.shape)

    solve(own[0:KEPT], 0)
    for c in SOLVE:
        if c:
            for i in range(KEPT):
                large["slab", c, i].wait()
            solve(land[c * KEPT : (c + 1) * KEPT], c * KEPT)
        else:
            for n in range(CP - KEPT):
                for copy in down_copies[n]:
                    copy.wait()
            solve(sums[0] + down[1] + down[2], W * KEPT)

    places.wait()
    blk = own.shape[1]
    for j in range(q_ref.shape[0] // blk):
        c, i = slot[j] // CP, lax.rem(slot[j], CP)
        q_ref[j * blk : (j + 1) * blk] = solved[jnp.where(i < KEPT, c * KEPT + i, W * KEPT + i - KEPT)]


def moved_and_solved(held, source_slot, total):
    bulk, wide = lax.axis_size("bulk"), lax.axis_size("wide")
    slots, blk, k = held.shape
    rest = CP - KEPT
    vmem, dma = pltpu.VMEM, pltpu.SemaphoreType.DMA
    return pl.pallas_call(
        functools.partial(window, bulk, wide, total),
        out_shape=[
            jax.ShapeDtypeStruct((source_slot.shape[0] * blk, k), F32),
            jax.ShapeDtypeStruct((k, k), F32),
        ],
        in_specs=[pl.BlockSpec(memory_space=pl.ANY)] * 2,
        out_specs=[pl.BlockSpec(memory_space=vmem)] * 2,
        scratch_shapes=[
            pltpu.SMEM(source_slot.shape, jnp.int32),
            dma((1,)),
            vmem((k, k), F32),
            vmem((W * KEPT + rest, blk, k), F32),
            vmem((slots, blk, k), F32),
            vmem((W * KEPT, blk, k), F32),
            vmem((bulk, k // bulk, k), F32),
            vmem((bulk, k // bulk, k), F32),
            vmem((CP, CP, k // bulk // CP, k), F32),
            vmem((wide // CP, k // bulk // CP, k), F32),
            vmem((CP, k // bulk // CP, k), F32),
            vmem((bulk, k // bulk, k), F32),
            vmem((k, k), F32),
            vmem((HALF, HALF), F32),
            vmem((HALF, HALF), F32),
            vmem((W, rest, blk, k), F32),
            vmem((3, rest, blk, k), F32),
            vmem((3, rest, blk, k), F32),
            vmem((k, k), BF16),
            vmem((k, k), BF16),
            dma((W,)), dma((bulk,)), dma((bulk,)), dma((CP,)), dma((CP,)), dma((wide // CP,)), dma((wide // CP,)),
            dma((CP,)), dma((CP,)), dma((bulk,)), dma((bulk,)),
            dma((W, KEPT)), dma((W, KEPT)), dma((W, KEPT)), dma((W, KEPT)), dma((3, rest)), dma((3, rest)),
        ],
        compiler_params=pltpu.CompilerParams(
            collective_id=0, has_side_effects=True, vmem_limit_bytes=VMEM
        ),
        name="window",
    )(source_slot, held)


def local(held, source_slot):
    total = lax.axis_size("bulk") * lax.axis_size("wide") * source_slot.shape[0] * held.shape[1]
    return tuple(moved_and_solved(held, source_slot, total))


def solution(mesh):
    in_specs = (P(("bulk", "wide"), None, None), P(("bulk", "wide")))
    out_specs = (P(("bulk", "wide"), None), P())
    return jax.shard_map(local, mesh=mesh, in_specs=in_specs, out_specs=out_specs, check_vma=False)
```

```python
import functools

import jax
import jax.numpy as jnp
from jax import lax
from jax.experimental import pallas as pl
from jax.experimental.pallas import tpu as pltpu
from jax.sharding import PartitionSpec as P

CP = 4
W = 8
KEPT = 2
def slabs(*cs):
    return tuple(("slab", c, 0) for c in cs)


def rows(i, *cs):
    return tuple(("row", c, i) for c in cs)


PLAN = (
    slabs(4) + rows(0, 1, 3),
    rows(0, 5, 7),
    slabs(7),
    rows(0, 2, 6) + rows(1, 1, 3, 5, 7) + slabs(6) + rows(1, 2, 6) + slabs(5, 3, 1, 2),
    (),
    (),
)
ROW_AT = (1, 2)
SOLVE = (7, 6, 5, 4, 3, 2, 1, 0)
VMEM = 50 * 2**20
MESH = pl.DeviceIdType.MESH
TILE = 8
HALF = 128
F32 = jnp.float32
BF16 = jnp.bfloat16


def row_of(x, r):
    return jnp.broadcast_to(x[r : r + 1, :], x.shape)


def col_of(x, c):
    return jnp.broadcast_to(x[:, c : c + 1], x.shape)


def reciprocal(x):
    y = pl.reciprocal(x, approx=True)
    return y * (2.0 - x * y)


def panels(a):
    count = HALF // TILE
    a = list(a)
    sub = lax.broadcasted_iota(jnp.int32, (TILE, HALF), 0)
    lane = lax.broadcasted_iota(jnp.int32, (TILE, HALF), 1)
    e = [jnp.where(lane == sub + TILE * t, 1.0, 0.0) for t in range(count)]
    upper, inverse = [], []
    for p in range(count):
        at = TILE * p
        cols = [col_of(a[p], at + q) for q in range(TILE)]
        d = {(i, j): row_of(cols[j], i) for i in range(TILE) for j in range(i, TILE)}
        y, z, l, inv = [], [], {}, []
        for r in range(TILE):
            yr, zr = row_of(a[p], r), row_of(e[p], r)
            for q in range(r):
                yr = yr - l[r, q] * y[q]
                zr = zr - l[r, q] * z[q]
            y.append(yr)
            z.append(zr)
            inv.append(reciprocal(d[r, r]))
            for i in range(r + 1, TILE):
                l[i, r] = d[r, i] * inv[r]
            for i in range(r + 1, TILE):
                for j in range(i, TILE):
                    d[i, j] = d[i, j] - l[i, r] * d[r, j]
        scale = lax.rsqrt(d[0, 0])
        rows_y, rows_z = y[0] * scale, z[0] * scale
        for r in range(1, TILE):
            scale = lax.rsqrt(d[r, r])
            rows_y = jnp.where(sub == r, y[r] * scale, rows_y)
            rows_z = jnp.where(sub == r, z[r] * scale, rows_z)
        upper.append(jnp.where(lane >= sub + at, rows_y, 0.0))
        inverse.append(jnp.where(lane <= sub + at, rows_z, 0.0))
        y = [y[r] * inv[r] for r in range(TILE)]
        z = [z[r] * inv[r] for r in range(TILE)]
        if p + 1 < count:
            c = [col_of(a[p + 1], at + q) for q in range(TILE)]
            for r in range(TILE):
                for q in range(r):
                    c[r] = c[r] - l[r, q] * c[q]
            for r in range(TILE):
                a[p + 1] = a[p + 1] - c[r] * y[r]
                e[p + 1] = e[p + 1] - c[r] * z[r]
        if p + 2 < count:
            for r in reversed(range(TILE)):
                for q in range(r + 1, TILE):
                    y[r] = y[r] - l[q, r] * y[q]
                    z[r] = z[r] - l[q, r] * z[q]
            for t in range(p + 2, count):
                c = [col_of(a[t], at + q) for q in range(TILE)]
                for r in range(TILE):
                    a[t] = a[t] - c[r] * y[r]
                    e[t] = e[t] - c[r] * z[r]
    return upper, inverse


def dot(x, y, over):
    return lax.dot_general(
        x, y, (over, ((), ())), precision=lax.Precision.HIGHEST, preferred_element_type=F32
    )


def split(x):
    high = x.astype(BF16)
    return high, (x - high.astype(F32)).astype(BF16)


def half_dot(x, y, over):
    return lax.dot_general(x, y, (over, ((), ())), preferred_element_type=F32)


def factored(gram, r_ref, w_ref, work, cross, between):
    n = HALF
    work[...] = gram[0:n, 0:n]
    r_ref[n:, 0:n] = jnp.zeros((n, n), F32)
    w_ref[0:n, n:] = jnp.zeros((n, n), F32)

    def half(h, carry):
        up, inv = panels([work[TILE * t : TILE * (t + 1), :] for t in range(n // TILE)])

        @pl.when(h == 0)
        def _():
            for t in range(n // TILE):
                r_ref[TILE * t : TILE * (t + 1), 0:n] = up[t]
                w_ref[TILE * t : TILE * (t + 1), 0:n] = inv[t]
            w = w_ref[0:n, 0:n]
            right = dot(w, gram[0:n, n:], ((1,), (0,)))
            r_ref[0:n, n:] = right
            work[...] = gram[n:, n:] - dot(right, right, ((0,), (0,)))
            cross[...] = dot(right, w, ((0,), (0,)))
            between()

        @pl.when(h == 1)
        def _():
            for t in range(n // TILE):
                r_ref[n + TILE * t : n + TILE * (t + 1), n:] = up[t]
                w_ref[n + TILE * t : n + TILE * (t + 1), n:] = inv[t]
            w_ref[n:, 0:n] = -dot(w_ref[n:, n:], cross[...], ((1,), (0,)))

        return carry

    lax.fori_loop(0, 2, half, 0)


def window(
    bulk, wide, total,
    slots, held, q_ref, r_ref,
    slot, slot_sem,     w_ref, solved, own, land, acc, parts, shares, columns, chunk, gram, flat, work, cross, across, sums, down, w_high, w_low,
    load_sem, part_send, part_recv, share_send, share_recv, column_send, column_recv, piece_send, piece_recv,
    gram_send, gram_recv, slab_send, slab_recv, row_send, row_recv, down_send, down_recv,
):
    my_bulk, my_wide = lax.axis_index("bulk"), lax.axis_index("wide")
    me = my_bulk * wide + my_wide
    devices = bulk * wide
    column, row = lax.rem(my_wide, CP), my_wide // CP
    height = wide // CP

    def along_bulk(o):
        return (lax.rem(my_bulk + o, bulk), my_wide)

    def behind(c):
        to = lax.rem(me + devices - c, devices)
        return (to // wide, lax.rem(to, wide))

    def in_row(b):
        return (my_bulk, row * CP + lax.rem(column + CP - b, CP))

    def in_column(b):
        return (my_bulk, lax.rem(row + height - b, height) * CP + column)

    def remote(src, dst, send, recv, to):
        return pltpu.make_async_remote_copy(
            src_ref=src, dst_ref=dst, send_sem=send, recv_sem=recv, device_id=to, device_id_type=MESH
        )

    barrier = pltpu.get_barrier_semaphore()
    far = [*range(1, W), 2 * CP]
    peers = [behind(devices - c) for c in far] + [in_row(b) for b in range(1, CP)]
    peers += [in_column(b) for b in range(1, height)] + [along_bulk(o) for o in range(1, bulk)]
    for peer in peers:
        pl.semaphore_signal(barrier, inc=1, device_id=peer, device_id_type=MESH)

    loads = [
        pltpu.make_async_copy(held.at[pl.ds(c * CP, CP)], own.at[pl.ds(c * CP, CP)], load_sem.at[c])
        for c in range(W)
    ]
    for load in loads:
        load.start()
    places = pltpu.make_async_copy(slots, slot, slot_sem.at[0])
    places.start()

    rows, k = CP * own.shape[1], own.shape[2]
    square, mixed = jnp.zeros((k, k), F32), jnp.zeros((k, k), F32)
    for c in range(W):
        loads[c].wait()
        high, low = split(own[c * CP : (c + 1) * CP].reshape(rows, k))
        square += half_dot(high, high, ((0,), (0,))) + half_dot(low, low, ((0,), (0,)))
        mixed += half_dot(high, low, ((0,), (0,)))
    acc[...] = (square + mixed + mixed.T).reshape(acc.shape)

    pl.semaphore_wait(barrier, len(peers))

    part_copies = [
        remote(acc.at[along_bulk(o)[0]], parts.at[o], part_send.at[o], part_recv.at[o], along_bulk(o))
        for o in range(1, bulk)
    ]
    for copy in part_copies:
        copy.start()

    large = {}
    for c in range(1, W):
        large["slab", c, 0] = remote(
            held.at[pl.ds(c * CP, KEPT)], land.at[pl.ds(c * KEPT, KEPT)], slab_send.at[c], slab_recv.at[c], behind(c)
        )
        if c % CP:
            for i in range(CP - KEPT):
                large["row", c, i] = remote(
                    held.at[c * CP + KEPT + i], across.at[c, i],
                    row_send.at[c, i], row_recv.at[c, i], in_row(c % CP),
                )

    def begin(point):
        for key in PLAN[point]:
            large[key].start()

    begin(0)

    part = acc[my_bulk]
    for o in range(1, bulk):
        part_copies[o - 1].wait_recv()
        part += parts[o]
    shares[0] = part.reshape(shares.shape[1:])
    share_copies = [
        remote(shares.at[0, lax.rem(column + CP - b, CP)], shares.at[b, 0], share_send.at[b], share_recv.at[b], in_row(b))
        for b in range(1, CP)
    ]
    for copy in share_copies:
        copy.start()
    begin(1)
    for copy in part_copies:
        copy.wait_send()
    share = shares[0, column]
    for b in range(1, CP):
        share_copies[b - 1].wait_recv()
        share += shares[b, 0]
    columns[row] = share
    column_copies = [
        remote(columns.at[row], columns.at[row], column_send.at[b], column_recv.at[b], in_column(b))
        for b in range(1, height)
    ]
    for copy in column_copies:
        copy.start()
    begin(2)
    for copy in share_copies:
        copy.wait_send()
    for copy in column_copies:
        copy.wait()
    share = columns[0]
    for b in range(1, height):
        share += columns[b]
    chunk[column] = share
    piece_copies = [
        remote(chunk.at[column], chunk.at[column], piece_send.at[b], piece_recv.at[b], in_row(b))
        for b in range(1, CP)
    ]
    for copy in piece_copies:
        copy.start()
    begin(3)
    for copy in piece_copies:
        copy.wait()
    gram[my_bulk] = chunk[...].reshape(gram.shape[1:])
    gram_copies = [
        remote(gram.at[my_bulk], gram.at[my_bulk], gram_send.at[o], gram_recv.at[o], along_bulk(o))
        for o in range(1, bulk)
    ]
    for copy in gram_copies:
        copy.start()
    begin(4)
    for copy in gram_copies:
        copy.wait()
    flat[...] = gram[...].reshape(k, k) / total

    begin(5)

    down_copies = [
        [
            remote(sums.at[i, n], down.at[i, n], down_send.at[i, n], down_recv.at[i, n], behind(CP * i))
            for i in (1, 2)
        ]
        for n in range(CP - KEPT)
    ]

    def next_row(n):
        for key, copy in large.items():
            if key[0] == "row" and key[2] == n:
                copy.wait()
        mine = [own[KEPT + n], own[CP * CP + KEPT + n], jnp.zeros(sums.shape[2:], F32)]
        for b in range(1, CP):
            near, far = across[b, n], across[b + CP, n]
            inside = column + b < CP
            mine[0] += jnp.where(inside, near, 0.0)
            mine[1] += jnp.where(inside, far, near)
            mine[2] += jnp.where(inside, 0.0, far)
        for i in range(3):
            sums[i, n] = mine[i]
        for copy in down_copies[n]:
            copy.start()

    def at_point(point):
        for n in range(CP - KEPT):
            if ROW_AT[n] == point:
                next_row(n)

    at_point(0)
    factored(flat, r_ref, w_ref, work, cross, functools.partial(at_point, 1))
    at_point(2)
    w_high[...], w_low[...] = split(w_ref[...])

    def solve(blocks, at):
        high, low = split(blocks.reshape(-1, k))
        over = ((1,), (1,))
        q = half_dot(low, w_high[...], over) + half_dot(high, w_low[...], over) + half_dot(high, w_high[...], over)
        solved[at : at + blocks.shape[0]] = q.reshape(blocks.shape)

    solve(own[0:KEPT], 0)
    for c in SOLVE:
        if c:
            large["slab", c, 0].wait()
            solve(land[c * KEPT : (c + 1) * KEPT], c * KEPT)
        else:
            for n in range(CP - KEPT):
                for copy in down_copies[n]:
                    copy.wait()
            solve(sums[0] + down[1] + down[2], W * KEPT)

    places.wait()
    blk = own.shape[1]
    for j in range(q_ref.shape[0] // blk):
        c, i = slot[j] // CP, lax.rem(slot[j], CP)
        q_ref[j * blk : (j + 1) * blk] = solved[jnp.where(i < KEPT, c * KEPT + i, W * KEPT + i - KEPT)]


def moved_and_solved(held, source_slot, total):
    bulk, wide = lax.axis_size("bulk"), lax.axis_size("wide")
    slots, blk, k = held.shape
    rest = CP - KEPT
    vmem, dma = pltpu.VMEM, pltpu.SemaphoreType.DMA
    return pl.pallas_call(
        functools.partial(window, bulk, wide, total),
        out_shape=[
            jax.ShapeDtypeStruct((source_slot.shape[0] * blk, k), F32),
            jax.ShapeDtypeStruct((k, k), F32),
        ],
        in_specs=[pl.BlockSpec(memory_space=pl.ANY)] * 2,
        out_specs=[pl.BlockSpec(memory_space=vmem)] * 2,
        scratch_shapes=[
            pltpu.SMEM(source_slot.shape, jnp.int32),
            dma((1,)),
            vmem((k, k), F32),
            vmem((W * KEPT + rest, blk, k), F32),
            vmem((slots, blk, k), F32),
            vmem((W * KEPT, blk, k), F32),
            vmem((bulk, k // bulk, k), F32),
            vmem((bulk, k // bulk, k), F32),
            vmem((CP, CP, k // bulk // CP, k), F32),
            vmem((wide // CP, k // bulk // CP, k), F32),
            vmem((CP, k // bulk // CP, k), F32),
            vmem((bulk, k // bulk, k), F32),
            vmem((k, k), F32),
            vmem((HALF, HALF), F32),
            vmem((HALF, HALF), F32),
            vmem((W, rest, blk, k), F32),
            vmem((3, rest, blk, k), F32),
            vmem((3, rest, blk, k), F32),
            vmem((k, k), BF16),
            vmem((k, k), BF16),
            dma((W,)), dma((bulk,)), dma((bulk,)), dma((CP,)), dma((CP,)), dma((wide // CP,)), dma((wide // CP,)),
            dma((CP,)), dma((CP,)), dma((bulk,)), dma((bulk,)),
            dma((W,)), dma((W,)), dma((W, rest)), dma((W, rest)), dma((3, rest)), dma((3, rest)),
        ],
        compiler_params=pltpu.CompilerParams(
            collective_id=0, has_side_effects=True, vmem_limit_bytes=VMEM
        ),
        name="window",
    )(source_slot, held)


def local(held, source_slot):
    total = lax.axis_size("bulk") * lax.axis_size("wide") * source_slot.shape[0] * held.shape[1]
    return tuple(moved_and_solved(held, source_slot, total))


def solution(mesh):
    in_specs = (P(("bulk", "wide"), None, None), P(("bulk", "wide")))
    out_specs = (P(("bulk", "wide"), None), P())
    return jax.shard_map(local, mesh=mesh, in_specs=in_specs, out_specs=out_specs, check_vma=False)
```

```python
import functools

import jax
import jax.numpy as jnp
from jax import lax
from jax.experimental import pallas as pl
from jax.experimental.pallas import tpu as pltpu
from jax.sharding import PartitionSpec as P

CP = 4
W = 8
KEPT = 2
def slabs(*cs):
    return tuple(("slab", c, 0) for c in cs)


def rows(i, *cs):
    return tuple(("row", c, i) for c in cs)


PLAN = (
    slabs(4) + rows(0, 1, 3),
    (),
    slabs(7),
    rows(0, 2) + rows(1, 1, 3, 2) + slabs(6, 5, 3, 2, 1),
    (),
    (),
)
ROW_AT = (1, 2)
SOLVE = (7, 6, 5, 4, 3, 2, 1, 0)
VMEM = 50 * 2**20
MESH = pl.DeviceIdType.MESH
TILE = 8
HALF = 128
F32 = jnp.float32
BF16 = jnp.bfloat16


def row_of(x, r):
    return jnp.broadcast_to(x[r : r + 1, :], x.shape)


def col_of(x, c):
    return jnp.broadcast_to(x[:, c : c + 1], x.shape)


def reciprocal(x):
    y = pl.reciprocal(x, approx=True)
    return y * (2.0 - x * y)


def panels(a):
    count = HALF // TILE
    a = list(a)
    sub = lax.broadcasted_iota(jnp.int32, (TILE, HALF), 0)
    lane = lax.broadcasted_iota(jnp.int32, (TILE, HALF), 1)
    e = [jnp.where(lane == sub + TILE * t, 1.0, 0.0) for t in range(count)]
    upper, inverse = [], []
    for p in range(count):
        at = TILE * p
        cols = [col_of(a[p], at + q) for q in range(TILE)]
        d = {(i, j): row_of(cols[j], i) for i in range(TILE) for j in range(i, TILE)}
        y, z, l, inv = [], [], {}, []
        for r in range(TILE):
            yr, zr = row_of(a[p], r), row_of(e[p], r)
            for q in range(r):
                yr = yr - l[r, q] * y[q]
                zr = zr - l[r, q] * z[q]
            y.append(yr)
            z.append(zr)
            inv.append(reciprocal(d[r, r]))
            for i in range(r + 1, TILE):
                l[i, r] = d[r, i] * inv[r]
            for i in range(r + 1, TILE):
                for j in range(i, TILE):
                    d[i, j] = d[i, j] - l[i, r] * d[r, j]
        scale = lax.rsqrt(d[0, 0])
        rows_y, rows_z = y[0] * scale, z[0] * scale
        for r in range(1, TILE):
            scale = lax.rsqrt(d[r, r])
            rows_y = jnp.where(sub == r, y[r] * scale, rows_y)
            rows_z = jnp.where(sub == r, z[r] * scale, rows_z)
        upper.append(jnp.where(lane >= sub + at, rows_y, 0.0))
        inverse.append(jnp.where(lane <= sub + at, rows_z, 0.0))
        y = [y[r] * inv[r] for r in range(TILE)]
        z = [z[r] * inv[r] for r in range(TILE)]
        if p + 1 < count:
            c = [col_of(a[p + 1], at + q) for q in range(TILE)]
            for r in range(TILE):
                for q in range(r):
                    c[r] = c[r] - l[r, q] * c[q]
            for r in range(TILE):
                a[p + 1] = a[p + 1] - c[r] * y[r]
                e[p + 1] = e[p + 1] - c[r] * z[r]
        if p + 2 < count:
            for r in reversed(range(TILE)):
                for q in range(r + 1, TILE):
                    y[r] = y[r] - l[q, r] * y[q]
                    z[r] = z[r] - l[q, r] * z[q]
            for t in range(p + 2, count):
                c = [col_of(a[t], at + q) for q in range(TILE)]
                for r in range(TILE):
                    a[t] = a[t] - c[r] * y[r]
                    e[t] = e[t] - c[r] * z[r]
    return upper, inverse


def dot(x, y, over):
    return lax.dot_general(
        x, y, (over, ((), ())), precision=lax.Precision.HIGHEST, preferred_element_type=F32
    )


def split(x):
    high = x.astype(BF16)
    return high, (x - high.astype(F32)).astype(BF16)


def half_dot(x, y, over):
    return lax.dot_general(x, y, (over, ((), ())), preferred_element_type=F32)


def factored(gram, r_ref, w_ref, work, cross, between):
    n = HALF
    work[...] = gram[0:n, 0:n]
    r_ref[n:, 0:n] = jnp.zeros((n, n), F32)
    w_ref[0:n, n:] = jnp.zeros((n, n), F32)

    def half(h, carry):
        up, inv = panels([work[TILE * t : TILE * (t + 1), :] for t in range(n // TILE)])

        @pl.when(h == 0)
        def _():
            for t in range(n // TILE):
                r_ref[TILE * t : TILE * (t + 1), 0:n] = up[t]
                w_ref[TILE * t : TILE * (t + 1), 0:n] = inv[t]
            w = w_ref[0:n, 0:n]
            right = dot(w, gram[0:n, n:], ((1,), (0,)))
            r_ref[0:n, n:] = right
            work[...] = gram[n:, n:] - dot(right, right, ((0,), (0,)))
            cross[...] = dot(right, w, ((0,), (0,)))
            between()

        @pl.when(h == 1)
        def _():
            for t in range(n // TILE):
                r_ref[n + TILE * t : n + TILE * (t + 1), n:] = up[t]
                w_ref[n + TILE * t : n + TILE * (t + 1), n:] = inv[t]
            w_ref[n:, 0:n] = -dot(w_ref[n:, n:], cross[...], ((1,), (0,)))

        return carry

    lax.fori_loop(0, 2, half, 0)


def window(
    bulk, wide, total,
    slots, held, q_ref, r_ref,
    slot, slot_sem,     w_ref, solved, own, land, acc, parts, shares, columns, chunk, gram, flat, work, cross, across, sums, down, w_high, w_low,
    load_sem, part_send, part_recv, share_send, share_recv, column_send, column_recv, piece_send, piece_recv,
    gram_send, gram_recv, slab_send, slab_recv, row_send, row_recv, down_send, down_recv,
):
    my_bulk, my_wide = lax.axis_index("bulk"), lax.axis_index("wide")
    me = my_bulk * wide + my_wide
    devices = bulk * wide
    column, row = lax.rem(my_wide, CP), my_wide // CP
    height = wide // CP

    def along_bulk(o):
        return (lax.rem(my_bulk + o, bulk), my_wide)

    def behind(c):
        to = lax.rem(me + devices - c, devices)
        return (to // wide, lax.rem(to, wide))

    def in_row(b):
        return (my_bulk, row * CP + lax.rem(column + CP - b, CP))

    def in_column(b):
        return (my_bulk, lax.rem(row + height - b, height) * CP + column)

    def remote(src, dst, send, recv, to):
        return pltpu.make_async_remote_copy(
            src_ref=src, dst_ref=dst, send_sem=send, recv_sem=recv, device_id=to, device_id_type=MESH
        )

    barrier = pltpu.get_barrier_semaphore()
    far = [*range(1, W), 2 * CP]
    peers = [behind(devices - c) for c in far] + [in_row(b) for b in range(1, CP)]
    peers += [in_column(b) for b in range(1, height)] + [along_bulk(o) for o in range(1, bulk)]
    for peer in peers:
        pl.semaphore_signal(barrier, inc=1, device_id=peer, device_id_type=MESH)

    loads = [
        pltpu.make_async_copy(held.at[c // CP, c % CP], own.at[pl.ds(c * CP, CP)], load_sem.at[c])
        for c in range(W)
    ]
    for load in loads:
        load.start()
    places = pltpu.make_async_copy(slots, slot, slot_sem.at[0])
    places.start()

    rows, k = CP * own.shape[1], own.shape[2]
    square, mixed = jnp.zeros((k, k), F32), jnp.zeros((k, k), F32)
    for c in range(W):
        loads[c].wait()
        high, low = split(own[c * CP : (c + 1) * CP].reshape(rows, k))
        square += half_dot(high, high, ((0,), (0,))) + half_dot(low, low, ((0,), (0,)))
        mixed += half_dot(high, low, ((0,), (0,)))
    acc[...] = (square + mixed + mixed.T).reshape(acc.shape)

    pl.semaphore_wait(barrier, len(peers))

    part_copies = [
        remote(acc.at[along_bulk(o)[0]], parts.at[o], part_send.at[o], part_recv.at[o], along_bulk(o))
        for o in range(1, bulk)
    ]
    for copy in part_copies:
        copy.start()

    large = {}
    for c in range(1, W):
        large["slab", c, 0] = remote(
            held.at[c // CP, c % CP, pl.ds(0, KEPT)], land.at[pl.ds(c * KEPT, KEPT)], slab_send.at[c], slab_recv.at[c], behind(c)
        )
        if c < CP:
            for i in range(CP - KEPT):
                large["row", c, i] = remote(
                    held.at[:, c, KEPT + i], across.at[c, i], row_send.at[c, i], row_recv.at[c, i], in_row(c)
                )

    def begin(point):
        for key in PLAN[point]:
            large[key].start()

    begin(0)

    part = acc[my_bulk]
    for o in range(1, bulk):
        part_copies[o - 1].wait_recv()
        part += parts[o]
    shares[0] = part.reshape(shares.shape[1:])
    share_copies = [
        remote(shares.at[0, lax.rem(column + CP - b, CP)], shares.at[b, 0], share_send.at[b], share_recv.at[b], in_row(b))
        for b in range(1, CP)
    ]
    for copy in share_copies:
        copy.start()
    begin(1)
    for copy in part_copies:
        copy.wait_send()
    share = shares[0, column]
    for b in range(1, CP):
        share_copies[b - 1].wait_recv()
        share += shares[b, 0]
    columns[row] = share
    column_copies = [
        remote(columns.at[row], columns.at[row], column_send.at[b], column_recv.at[b], in_column(b))
        for b in range(1, height)
    ]
    for copy in column_copies:
        copy.start()
    begin(2)
    for copy in share_copies:
        copy.wait_send()
    for copy in column_copies:
        copy.wait()
    share = columns[0]
    for b in range(1, height):
        share += columns[b]
    chunk[column] = share
    piece_copies = [
        remote(chunk.at[column], chunk.at[column], piece_send.at[b], piece_recv.at[b], in_row(b))
        for b in range(1, CP)
    ]
    for copy in piece_copies:
        copy.start()
    begin(3)
    for copy in piece_copies:
        copy.wait()
    gram[my_bulk] = chunk[...].reshape(gram.shape[1:])
    gram_copies = [
        remote(gram.at[my_bulk], gram.at[my_bulk], gram_send.at[o], gram_recv.at[o], along_bulk(o))
        for o in range(1, bulk)
    ]
    for copy in gram_copies:
        copy.start()
    begin(4)
    for copy in gram_copies:
        copy.wait()
    flat[...] = gram[...].reshape(k, k) / total

    begin(5)

    down_copies = [
        [
            remote(sums.at[i, n], down.at[i, n], down_send.at[i, n], down_recv.at[i, n], behind(CP * i))
            for i in (1, 2)
        ]
        for n in range(CP - KEPT)
    ]

    def next_row(n):
        for key, copy in large.items():
            if key[0] == "row" and key[2] == n:
                copy.wait()
        mine = [own[KEPT + n], own[CP * CP + KEPT + n], jnp.zeros(sums.shape[2:], F32)]
        for b in range(1, CP):
            near, far = across[b, n, 0], across[b, n, 1]
            inside = column + b < CP
            mine[0] += jnp.where(inside, near, 0.0)
            mine[1] += jnp.where(inside, far, near)
            mine[2] += jnp.where(inside, 0.0, far)
        for i in range(3):
            sums[i, n] = mine[i]
        for copy in down_copies[n]:
            copy.start()

    def at_point(point):
        for n in range(CP - KEPT):
            if ROW_AT[n] == point:
                next_row(n)

    at_point(0)
    factored(flat, r_ref, w_ref, work, cross, functools.partial(at_point, 1))
    at_point(2)
    w_high[...], w_low[...] = split(w_ref[...])

    def solve(blocks, at):
        high, low = split(blocks.reshape(-1, k))
        over = ((1,), (1,))
        q = half_dot(low, w_high[...], over) + half_dot(high, w_low[...], over) + half_dot(high, w_high[...], over)
        solved[at : at + blocks.shape[0]] = q.reshape(blocks.shape)

    solve(own[0:KEPT], 0)
    for c in SOLVE:
        if c:
            large["slab", c, 0].wait()
            solve(land[c * KEPT : (c + 1) * KEPT], c * KEPT)
        else:
            for n in range(CP - KEPT):
                for copy in down_copies[n]:
                    copy.wait()
            solve(sums[0] + down[1] + down[2], W * KEPT)

    places.wait()
    blk = own.shape[1]
    for j in range(q_ref.shape[0] // blk):
        c, i = slot[j] // CP, lax.rem(slot[j], CP)
        q_ref[j * blk : (j + 1) * blk] = solved[jnp.where(i < KEPT, c * KEPT + i, W * KEPT + i - KEPT)]


def moved_and_solved(held, source_slot, total):
    bulk, wide = lax.axis_size("bulk"), lax.axis_size("wide")
    slots, blk, k = held.shape
    rest = CP - KEPT
    vmem, dma = pltpu.VMEM, pltpu.SemaphoreType.DMA
    return pl.pallas_call(
        functools.partial(window, bulk, wide, total),
        out_shape=[
            jax.ShapeDtypeStruct((source_slot.shape[0] * blk, k), F32),
            jax.ShapeDtypeStruct((k, k), F32),
        ],
        in_specs=[pl.BlockSpec(memory_space=pl.ANY)] * 2,
        out_specs=[pl.BlockSpec(memory_space=vmem)] * 2,
        scratch_shapes=[
            pltpu.SMEM(source_slot.shape, jnp.int32),
            dma((1,)),
            vmem((k, k), F32),
            vmem((W * KEPT + rest, blk, k), F32),
            vmem((slots, blk, k), F32),
            vmem((W * KEPT, blk, k), F32),
            vmem((bulk, k // bulk, k), F32),
            vmem((bulk, k // bulk, k), F32),
            vmem((CP, CP, k // bulk // CP, k), F32),
            vmem((wide // CP, k // bulk // CP, k), F32),
            vmem((CP, k // bulk // CP, k), F32),
            vmem((bulk, k // bulk, k), F32),
            vmem((k, k), F32),
            vmem((HALF, HALF), F32),
            vmem((HALF, HALF), F32),
            vmem((CP, rest, W // CP, blk, k), F32),
            vmem((3, rest, blk, k), F32),
            vmem((3, rest, blk, k), F32),
            vmem((k, k), BF16),
            vmem((k, k), BF16),
            dma((W,)), dma((bulk,)), dma((bulk,)), dma((CP,)), dma((CP,)), dma((wide // CP,)), dma((wide // CP,)),
            dma((CP,)), dma((CP,)), dma((bulk,)), dma((bulk,)),
            dma((W,)), dma((W,)), dma((CP, rest)), dma((CP, rest)), dma((3, rest)), dma((3, rest)),
        ],
        compiler_params=pltpu.CompilerParams(
            collective_id=0, has_side_effects=True, vmem_limit_bytes=VMEM
        ),
        name="window",
    )(source_slot, held.reshape(W // CP, CP, CP, blk, k))


def local(held, source_slot):
    total = lax.axis_size("bulk") * lax.axis_size("wide") * source_slot.shape[0] * held.shape[1]
    return tuple(moved_and_solved(held, source_slot, total))


def solution(mesh):
    in_specs = (P(("bulk", "wide"), None, None), P(("bulk", "wide")))
    out_specs = (P(("bulk", "wide"), None), P())
    return jax.shard_map(local, mesh=mesh, in_specs=in_specs, out_specs=out_specs, check_vma=False)
```
